32 devices in a mesh: groups: 2 (over y), tile: 4 (over z), col: 2 (over x), branch: 2 (over core).
Axes of the slice: x: 2, y: 2, z: 4, core: 2. Of those that a mesh axis runs over, the one named last changes fastest.
Arguments:
- alignment_tensor: float32 [4, 64, 256, 256], P(('groups', 'branch'), 'tile', 'col'), parts along dimension 0, may hold values from -6 to 6
- residue_grid: float32 [4, 256, 256, 128], P(('groups', 'branch'), 'tile', 'col'), parts along dimension 0, may hold values from -6 to 6
- mixing_scale_vector: float32 [256], replicated, may hold values from 0.1 to 1.9
- logit_offset_scale: float32 [128], replicated, may hold values from 0.1 to 1.9
- feedforward_scale: float32 [256], replicated, may hold values from 0.1 to 1.9
- product_scale_vector: float32 [256], replicated, may hold values from 0.1 to 1.9
- grid_scale_vector: float32 [128], replicated, may hold values from 0.1 to 1.9
- logit_offset_map: float32 [128, 8], replicated, may hold values from -0.5 to 0.5
- asking_mapping: bfloat16 [256, 256], replicated, may hold values from -0.375 to 0.375
- lookup_mapping: bfloat16 [256, 256], replicated, may hold values from -0.375 to 0.375
- content_mapping: bfloat16 [256, 256], replicated, may hold values from -0.375 to 0.375
- mixing_return_matrix: bfloat16 [256, 256], replicated, may hold values from -0.375 to 0.375
- alignment_widen_map: bfloat16 [256, 1024], replicated, may hold values from -0.375 to 0.375
- alignment_shrink_map: bfloat16 [1024, 256], replicated, may hold values from -0.1875 to 0.1875
- former_embedding_map: bfloat16 [256, 32], replicated, may hold values from -0.375 to 0.375
- latter_embedding_map: bfloat16 [256, 32], replicated, may hold values from -0.375 to 0.375
- product_return_map: float32 [1024, 128], replicated, may hold values from -1 to 1
- grid_widen_map: bfloat16 [128, 512], replicated, may hold values from -0.5 to 0.5
- grid_shrink_map: bfloat16 [512, 128], replicated, may hold values from -0.25 to 0.25
Outputs:
- alignment_revised: float32 [4, 64, 256, 256], P(('groups', 'branch'), 'tile', 'col'), parts along dimension 0
- grid_revised: float32 [4, 256, 256, 128], P(('groups', 'branch'), 'tile', 'col'), parts along dimension 0
The draws below stay inside these ranges and needn't reach their ends.
There are 2 independent parts, one for each index of `groups`. The reference program is written for one: setup_inputs(seed, part) draws one part's arguments, and reference() takes and returns one part's arrays. A program takes and returns all parts, laid end to end along the dimension named above; an argument that names none is the same for every part. Nothing has to cross between parts.
All inputs are finite; a program needn't handle non-finite values.
Results may differ from the reference program's by a relative error of at most 0.0075.
Values may be sent and summed in bfloat16 or wider, within the bound.
A program may use at most 128 MiB of HBM per device.

```python
import jax
import jax.numpy as jnp
from jax import lax

ALIGN_FEATURES = 256
CZ = 128
HEADS = 8
TENSOR_FEATURES = 32
ALIGN_EXPANDED = 1024
PAIR_FF = 512
SEQUENCE_DEPTH = 64
CHAIN_LENGTH = 256
SAMPLE_TOTAL = 2


def levels(own_key, dims, split, low, top_value):
    def one(dim, parts):
        draws = jax.random.uniform(jax.random.fold_in(jax.random.fold_in(own_key, 6), dim), (parts,), jnp.float32, low / len(split), top_value / len(split))
        return jnp.repeat(jnp.exp(draws), dims[dim] // parts).reshape((-1,) + (1,) * (len(dims) - dim - 1))

    level = one(*split[0])
    for cut in split[1:]:
        level = level * one(*cut)
    return level


def gaussian(key, shape, scale, most, cuts=(), dtype=jnp.bfloat16):
    factor_of = levels(key, shape, cuts, -0.22, 0.18) if cuts else 1.0
    drawn = jax.random.normal(key, shape, jnp.float32) * scale * factor_of
    return jnp.minimum(jnp.maximum(drawn, -most), most).astype(dtype)


def setup_inputs(seed: int = 0, part: int = 0) -> dict:
    seeds = jax.random.split(jax.random.key(seed), 20)
    part_splits = jax.random.split(jax.random.fold_in(seeds[19], part), 20)
    alignment_tensor = gaussian(part_splits[0], (SAMPLE_TOTAL, SEQUENCE_DEPTH, CHAIN_LENGTH, ALIGN_FEATURES), 1.0, 6.0, ((0, 2), (1, 4), (2, 2)), jnp.float32)
    residue_grid = gaussian(part_splits[1], (SAMPLE_TOTAL, CHAIN_LENGTH, CHAIN_LENGTH, CZ), 1.0, 6.0, ((0, 2), (1, 4), (2, 2)), jnp.float32)
    mixing_scale_vector = jnp.clip(1.0 + 0.18 * jax.random.normal(seeds[2], (ALIGN_FEATURES,), jnp.float32), 0.1, 1.9)
    logit_offset_scale = jnp.clip(1.0 + 0.18 * jax.random.normal(seeds[3], (CZ,), jnp.float32), 0.1, 1.9)
    feedforward_scale = jnp.clip(1.0 + 0.18 * jax.random.normal(seeds[4], (ALIGN_FEATURES,), jnp.float32), 0.1, 1.9)
    product_scale_vector = jnp.clip(1.0 + 0.18 * jax.random.normal(seeds[5], (ALIGN_FEATURES,), jnp.float32), 0.1, 1.9)
    grid_scale_vector = jnp.clip(1.0 + 0.18 * jax.random.normal(seeds[6], (CZ,), jnp.float32), 0.1, 1.9)
    logit_offset_map = gaussian(seeds[7], (CZ, HEADS), CZ ** -0.5, 0.5, (), jnp.float32)
    asking_mapping = gaussian(seeds[8], (ALIGN_FEATURES, ALIGN_FEATURES), ALIGN_FEATURES ** -0.5, 0.375)
    lookup_mapping = gaussian(seeds[9], (ALIGN_FEATURES, ALIGN_FEATURES), ALIGN_FEATURES ** -0.5, 0.375)
    content_mapping = gaussian(seeds[10], (ALIGN_FEATURES, ALIGN_FEATURES), ALIGN_FEATURES ** -0.5, 0.375)
    mixing_return_matrix = gaussian(seeds[11], (ALIGN_FEATURES, ALIGN_FEATURES), ALIGN_FEATURES ** -0.5, 0.375)
    alignment_widen_map = gaussian(seeds[12], (ALIGN_FEATURES, ALIGN_EXPANDED), ALIGN_FEATURES ** -0.5, 0.375)
    alignment_shrink_map = gaussian(seeds[13], (ALIGN_EXPANDED, ALIGN_FEATURES), ALIGN_EXPANDED ** -0.5, 0.1875)
    former_embedding_map = gaussian(seeds[14], (ALIGN_FEATURES, TENSOR_FEATURES), ALIGN_FEATURES ** -0.5, 0.375)
    latter_embedding_map = gaussian(seeds[15], (ALIGN_FEATURES, TENSOR_FEATURES), ALIGN_FEATURES ** -0.5, 0.375)
    product_return_map = gaussian(seeds[16], (TENSOR_FEATURES * TENSOR_FEATURES, CZ), TENSOR_FEATURES ** -0.5, 1.0, (), jnp.float32)
    grid_widen_map = gaussian(seeds[17], (CZ, PAIR_FF), CZ ** -0.5, 0.5)
    grid_shrink_map = gaussian(seeds[18], (PAIR_FF, CZ), PAIR_FF ** -0.5, 0.25)
    return dict(alignment_tensor=alignment_tensor, residue_grid=residue_grid, mixing_scale_vector=mixing_scale_vector, logit_offset_scale=logit_offset_scale, feedforward_scale=feedforward_scale, product_scale_vector=product_scale_vector, grid_scale_vector=grid_scale_vector, logit_offset_map=logit_offset_map, asking_mapping=asking_mapping, lookup_mapping=lookup_mapping, content_mapping=content_mapping, mixing_return_matrix=mixing_return_matrix, alignment_widen_map=alignment_widen_map, alignment_shrink_map=alignment_shrink_map, former_embedding_map=former_embedding_map, latter_embedding_map=latter_embedding_map, product_return_map=product_return_map, grid_widen_map=grid_widen_map, grid_shrink_map=grid_shrink_map)


def standardize_features(x, gain):
    mean = lax.optimization_barrier(jnp.mean(x, axis=-1, keepdims=True))
    var = lax.optimization_barrier(jnp.mean((x - mean) ** 2, axis=-1, keepdims=True))
    return (x - mean) * lax.rsqrt(var + 1e-05) * gain

def lone_sample(alignment_tensor, residue_grid, mixing_scale_vector, logit_offset_scale, feedforward_scale, product_scale_vector, grid_scale_vector, logit_offset_map, asking_mapping, lookup_mapping, content_mapping, mixing_return_matrix, alignment_widen_map, alignment_shrink_map, former_embedding_map, latter_embedding_map, product_return_map, grid_widen_map, grid_shrink_map):
    subspace_total = logit_offset_map.shape[1]
    feature_extent = alignment_tensor.shape[-1]
    subspace_number = feature_extent // subspace_total
    bias = jnp.einsum('ijc,ch->hij', standardize_features(residue_grid, logit_offset_scale), logit_offset_map, precision=lax.Precision.HIGHEST)
    standardized_source = standardize_features(alignment_tensor, mixing_scale_vector).astype(jnp.bfloat16)
    asking_vectors = jnp.dot(standardized_source, asking_mapping, preferred_element_type=jnp.float32).astype(jnp.bfloat16)
    lookup_vectors = jnp.dot(standardized_source, lookup_mapping, preferred_element_type=jnp.float32).astype(jnp.bfloat16)
    content_vectors = jnp.dot(standardized_source, content_mapping, preferred_element_type=jnp.float32).astype(jnp.bfloat16)
    sample_portion = min(16, SEQUENCE_DEPTH)
    reformed = (SEQUENCE_DEPTH // sample_portion, sample_portion, CHAIN_LENGTH, subspace_total, subspace_number)

    def gated_softmax_mixing(items):
        qpart, kpart, vpart = items
        scores = jnp.einsum('sqhd,skhd->shqk', qpart.astype(jnp.float32), kpart.astype(jnp.float32)) / jnp.sqrt(jnp.float32(subspace_number)) + bias[None]
        weights = jax.nn.softmax(scores, axis=-1).astype(jnp.bfloat16)
        mixed = jnp.einsum('shqk,skhd->sqhd', weights.astype(jnp.float32), vpart.astype(jnp.float32))
        return mixed.astype(jnp.bfloat16).reshape(sample_portion, CHAIN_LENGTH, feature_extent)
    mixing_outcome = lax.map(gated_softmax_mixing, (asking_vectors.reshape(reformed), lookup_vectors.reshape(reformed), content_vectors.reshape(reformed))).reshape(SEQUENCE_DEPTH, CHAIN_LENGTH, feature_extent)
    alignment_activations = alignment_tensor + jnp.dot(mixing_outcome, mixing_return_matrix, preferred_element_type=jnp.float32)
    expanded_features = jax.nn.relu(jnp.dot(standardize_features(alignment_activations, feedforward_scale).astype(jnp.bfloat16), alignment_widen_map, preferred_element_type=jnp.float32)).astype(jnp.bfloat16)
    alignment_revised = alignment_activations + jnp.dot(expanded_features, alignment_shrink_map, preferred_element_type=jnp.float32)
    product_operands = standardize_features(alignment_tensor, product_scale_vector).astype(jnp.bfloat16)
    former_tensor = jnp.dot(product_operands, former_embedding_map, preferred_element_type=jnp.float32).astype(jnp.bfloat16)
    latter_tensor = jnp.dot(product_operands, latter_embedding_map, preferred_element_type=jnp.float32).astype(jnp.bfloat16)
    product_extent = former_tensor.shape[-1]
    latter_portion = min(16, CHAIN_LENGTH)
    former_portions = former_tensor.reshape(SEQUENCE_DEPTH, CHAIN_LENGTH // latter_portion, latter_portion, product_extent).transpose(1, 0, 2, 3)

    def outer_rows(fragment):
        tensor_product = jnp.einsum('era,eyq->ryaq', fragment.astype(jnp.float32), latter_tensor.astype(jnp.float32)) / SEQUENCE_DEPTH
        return jnp.dot(tensor_product.reshape(latter_portion, CHAIN_LENGTH, product_extent * product_extent), product_return_map, precision=lax.Precision.HIGHEST)
    update = lax.map(outer_rows, former_portions).reshape(CHAIN_LENGTH, CHAIN_LENGTH, -1)
    pair_mid = residue_grid + update
    spread = jax.nn.relu(jnp.dot(standardize_features(pair_mid, grid_scale_vector).astype(jnp.bfloat16), grid_widen_map, preferred_element_type=jnp.float32)).astype(jnp.bfloat16)
    grid_revised = pair_mid + jnp.dot(spread, grid_shrink_map, preferred_element_type=jnp.float32)
    return (alignment_revised, grid_revised)

def reference(alignment_tensor, residue_grid, mixing_scale_vector, logit_offset_scale, feedforward_scale, product_scale_vector, grid_scale_vector, logit_offset_map, asking_mapping, lookup_mapping, content_mapping, mixing_return_matrix, alignment_widen_map, alignment_shrink_map, former_embedding_map, latter_embedding_map, product_return_map, grid_widen_map, grid_shrink_map):
    alignment_samples = []
    grid_samples = []
    for sample_number in range(SAMPLE_TOTAL):
        former_embedding, latter_embedding = lone_sample(alignment_tensor[sample_number], residue_grid[sample_number], mixing_scale_vector, logit_offset_scale, feedforward_scale, product_scale_vector, grid_scale_vector, logit_offset_map, asking_mapping, lookup_mapping, content_mapping, mixing_return_matrix, alignment_widen_map, alignment_shrink_map, former_embedding_map, latter_embedding_map, product_return_map, grid_widen_map, grid_shrink_map)
        alignment_samples.append(former_embedding)
        grid_samples.append(latter_embedding)
    return (jnp.stack(alignment_samples), jnp.stack(grid_samples))
```

```python
import functools

import jax
import jax.numpy as jnp
from jax import lax
from jax.experimental import pallas as pl
from jax.experimental.pallas import tpu as pltpu
from jax.sharding import PartitionSpec as P

SEQUENCE_DEPTH = 64


def standardize_features(x, gain):
    mean = jnp.mean(x, axis=-1, keepdims=True)
    var = jnp.mean((x - mean) ** 2, axis=-1, keepdims=True)
    return (x - mean) * lax.rsqrt(var + 1e-05) * gain


def plain_device(
    alignment_tensor,
    residue_grid,
    mixing_scale_vector,
    logit_offset_scale,
    feedforward_scale,
    product_scale_vector,
    grid_scale_vector,
    logit_offset_map,
    asking_mapping,
    lookup_mapping,
    content_mapping,
    mixing_return_matrix,
    alignment_widen_map,
    alignment_shrink_map,
    former_embedding_map,
    latter_embedding_map,
    product_return_map,
    grid_widen_map,
    grid_shrink_map,
):
    sample_alignment = alignment_tensor[0]
    local_pair = residue_grid[0]
    subspace_total = logit_offset_map.shape[1]
    feature_extent = sample_alignment.shape[-1]
    subspace_number = feature_extent // subspace_total
    sequences_available = sample_alignment.shape[0]
    chain_available = sample_alignment.shape[1]
    tile_rows = local_pair.shape[0]
    tile_cols = local_pair.shape[1]
    product_extent = former_embedding_map.shape[1]
    product_operands = standardize_features(sample_alignment, product_scale_vector).astype(
        jnp.bfloat16
    )
    former_tensor = jnp.dot(
        product_operands, former_embedding_map, preferred_element_type=jnp.float32
    ).astype(jnp.bfloat16)
    latter_tensor = jnp.dot(
        product_operands, latter_embedding_map, preferred_element_type=jnp.float32
    ).astype(jnp.bfloat16)
    left_rows, right_rows = (
        lax.all_gather(former_tensor, "tile", axis=0, tiled=True),
        lax.all_gather(latter_tensor, "tile", axis=0, tiled=True),
    )
    left_all = lax.all_gather(left_rows, "col", axis=1, tiled=True)
    left_mine = lax.dynamic_slice_in_dim(left_all, lax.axis_index("tile") * tile_rows, tile_rows, 1)
    tensor_product = (
        jnp.einsum("era,eyq->ryaq", left_mine, right_rows, preferred_element_type=jnp.float32)
        / SEQUENCE_DEPTH
    )
    update = jnp.dot(
        tensor_product.reshape(tile_rows, tile_cols, product_extent * product_extent),
        product_return_map,
        precision=lax.Precision.HIGHEST,
    )
    bias_tile = jnp.einsum(
        "ijc,ch->hij",
        standardize_features(local_pair, logit_offset_scale),
        logit_offset_map,
        precision=lax.Precision.HIGHEST,
    )
    wide = lax.all_gather(bias_tile, "col", axis=2, tiled=True)
    whole = lax.all_gather(wide.astype(jnp.bfloat16), "tile", axis=1, tiled=True).astype(wide.dtype)
    bias = lax.dynamic_slice_in_dim(
        whole, lax.axis_index("col") * chain_available, chain_available, 1
    )
    standardized_source = standardize_features(sample_alignment, mixing_scale_vector).astype(
        jnp.bfloat16
    )
    asking_vectors = jnp.dot(
        standardized_source, asking_mapping, preferred_element_type=jnp.float32
    ).astype(jnp.bfloat16)
    lookup_vectors = jnp.dot(
        standardized_source, lookup_mapping, preferred_element_type=jnp.float32
    ).astype(jnp.bfloat16)
    content_vectors = jnp.dot(
        standardized_source, content_mapping, preferred_element_type=jnp.float32
    ).astype(jnp.bfloat16)
    all_keys, all_values = (
        lax.all_gather(lookup_vectors, "col", axis=1, tiled=True),
        lax.all_gather(content_vectors, "col", axis=1, tiled=True),
    )
    total_res = all_keys.shape[1]
    asking_vectors = asking_vectors.reshape(
        sequences_available, chain_available, subspace_total, subspace_number
    )
    all_keys = all_keys.reshape(sequences_available, total_res, subspace_total, subspace_number)
    all_values = all_values.reshape(sequences_available, total_res, subspace_total, subspace_number)
    scores = (
        jnp.einsum("sqhd,skhd->shqk", asking_vectors, all_keys, preferred_element_type=jnp.float32)
        / jnp.sqrt(jnp.float32(subspace_number))
        + bias[None]
    )
    weights = jax.nn.softmax(scores, axis=-1).astype(jnp.bfloat16)
    mixing_outcome = jnp.einsum(
        "shqk,skhd->sqhd", weights, all_values, preferred_element_type=jnp.float32
    )
    mixing_outcome = mixing_outcome.astype(jnp.bfloat16).reshape(
        sequences_available, chain_available, feature_extent
    )
    alignment_activations = sample_alignment + jnp.dot(
        mixing_outcome, mixing_return_matrix, preferred_element_type=jnp.float32
    )
    expanded_features = jax.nn.relu(
        jnp.dot(
            standardize_features(alignment_activations, feedforward_scale).astype(jnp.bfloat16),
            alignment_widen_map,
            preferred_element_type=jnp.float32,
        )
    ).astype(jnp.bfloat16)
    alignment_revised = alignment_activations + jnp.dot(
        expanded_features, alignment_shrink_map, preferred_element_type=jnp.float32
    )
    pair_mid = local_pair + update
    spread = jax.nn.relu(
        jnp.dot(
            standardize_features(pair_mid, grid_scale_vector).astype(jnp.bfloat16),
            grid_widen_map,
            preferred_element_type=jnp.float32,
        )
    ).astype(jnp.bfloat16)
    grid_revised = pair_mid + jnp.dot(spread, grid_shrink_map, preferred_element_type=jnp.float32)
    return (alignment_revised[None], grid_revised[None])


BF = jnp.bfloat16
F32 = jnp.float32
LANES = 128
LOG2E = 1.4426950408889634
MESH = pl.DeviceIdType.MESH


def center(x):
    mean = jnp.mean(x, axis=-1, keepdims=True)
    d = x - mean
    return d * lax.rsqrt(jnp.mean(d * d, axis=-1, keepdims=True) + 1e-05)


def dot(a, b, ca=1, cb=0):
    return lax.dot_general(a, b, (((ca,), (cb,)), ((), ())), preferred_element_type=F32)


def exchange_kernel(
    tiles,
    cols,
    x_ref,
    pair_ref,
    gm_ref,
    gp_ref,
    gb_ref,
    mapt_ref,
    wlt_ref,
    wrt_ref,
    normed_ref,
    left_ref,
    right_ref,
    bias_ref,
    y_ref,
    lmine,
    bmine,
    wl4,
    send_x,
    recv_x,
    send_l,
    recv_l,
    send_r,
    recv_r,
    send_b,
    recv_b,
):
    t = lax.axis_index("tile")
    c = lax.axis_index("col")
    n = tiles // cols
    rows, res, feat = x_ref.shape
    trows, tcols, cz = pair_ref.shape
    prod = wlt_ref.shape[0]
    pack = LANES // prod
    barrier = pltpu.get_barrier_semaphore()
    for dt in range(tiles):
        for dc in range(cols):
            if dt or dc:
                pl.semaphore_signal(
                    barrier,
                    inc=1,
                    device_id={
                        "tile": lax.rem(t + dt, tiles),
                        "col": lax.rem(c + dc, cols),
                    },
                    device_id_type=MESH,
                )

    wlt = wlt_ref[...]
    wl4[...] = jnp.zeros_like(wl4)
    for r in range(pack):
        wl4[r, r * prod : (r + 1) * prod, :] = wlt
    gp = gp_ref[...]
    gm = gm_ref[...]
    own = normed_ref.at[c]
    chunks = feat // LANES

    def factor(w, s, at):
        parts = [y_ref[(f, s) + at].astype(BF) for f in range(chunks)]
        return dot(w, jnp.concatenate(parts, axis=1), 1, 1)

    def rows_body(s, carry):
        z = center(x_ref[s])
        y = z * gp
        for f in range(chunks):
            y_ref[f, s, :, :] = y[:, f * LANES : (f + 1) * LANES]
        own[s, :, :] = (z * gm).astype(BF)
        return carry

    lax.fori_loop(0, rows, rows_body, 0)

    group = 16
    for s0 in range(0, rows, group):
        right = jnp.stack(
            [factor(wrt_ref[...], s, ()) for s in range(s0, s0 + group)]
        )
        right_ref[t, :, s0 : s0 + group, :] = jnp.swapaxes(right, 0, 1).astype(BF)
        left = []
        for s in range(s0, s0 + group):
            acc = None
            for r in range(pack):
                at = (pl.ds(r, res // pack, stride=pack), slice(None))
                parts = [y_ref[(f, s) + at].astype(BF) for f in range(chunks)]
                part = dot(jnp.concatenate(parts, axis=1), wl4[r], 1, 1)
                acc = part if acc is None else acc + part
            left.append(acc)
        lmine[:, s0 : s0 + group, :] = jnp.swapaxes(jnp.stack(left), 0, 1).astype(BF)

    pl.semaphore_wait(barrier, tiles * cols - 1)

    piece = trows // pack

    def left_copy(k, c2):
        dest = c * n + k
        src = lmine.at[pl.ds(k * piece, piece)]
        i = k * cols + c2
        away = jnp.logical_or(dest != t, c != c2)
        remote = pltpu.make_async_remote_copy(
            src_ref=src,
            dst_ref=left_ref.at[t],
            send_sem=send_l.at[i],
            recv_sem=recv_l.at[t],
            device_id={"tile": dest, "col": c2},
            device_id_type=MESH,
        )
        local = pltpu.make_async_copy(src, left_ref.at[t], recv_l.at[t])
        return away, remote, local

    def bias_copy(t2):
        owner = t // n
        slot = bias_ref.at[lax.rem(t, n), c]
        sem = recv_b.at[lax.rem(t, n) * cols + c]
        away = jnp.logical_or(t2 != t, c != owner)
        remote = pltpu.make_async_remote_copy(
            src_ref=bmine,
            dst_ref=slot,
            send_sem=send_b.at[t2],
            recv_sem=sem,
            device_id={"tile": t2, "col": owner},
            device_id_type=MESH,
        )
        local = pltpu.make_async_copy(bmine, slot, sem)
        return away, remote, local

    def start(copy):
        away, remote, local = copy

        @pl.when(away)
        def _():
            remote.start()

        @pl.when(jnp.logical_not(away))
        def _():
            local.start()

    def finish(copy):
        away, remote, _ = copy

        @pl.when(away)
        def _():
            remote.wait_send()

    def right_copy(dt):
        return pltpu.make_async_remote_copy(
            src_ref=right_ref.at[t],
            dst_ref=right_ref.at[t],
            send_sem=send_r.at[dt],
            recv_sem=recv_r.at[t],
            device_id={"tile": lax.rem(t + dt, tiles)},
            device_id_type=MESH,
        )

    def normed_copy(dc):
        return pltpu.make_async_remote_copy(
            src_ref=own,
            dst_ref=own,
            send_sem=send_x.at[dc],
            recv_sem=recv_x.at[c],
            device_id={"col": lax.rem(c + dc, cols)},
            device_id_type=MESH,
        )

    lefts = [left_copy(k, c2) for k in range(n) for c2 in range(cols)]
    for copy in lefts:
        start(copy)
    for dt in range(1, tiles):
        right_copy(dt).start()
    for dc in range(1, cols):
        normed_copy(dc).start()

    mapt = mapt_ref[...] * gb_ref[...]
    high = mapt.astype(BF)
    low = (mapt - high.astype(F32)).astype(BF)
    both = jnp.concatenate([high.astype(F32), low.astype(F32)], axis=0).astype(BF)
    heads = mapt.shape[0]
    ib = 16

    def bias_body(b, carry):
        z = center(pair_ref[pl.ds(b * ib, ib)]).astype(BF)
        out = []
        for i in range(ib):
            p = dot(both, z[i], 1, 1)
            out.append(p[:heads] + p[heads:])
        bmine[:, pl.ds(pl.multiple_of(b * ib, ib), ib), :] = jnp.swapaxes(
            jnp.stack(out), 0, 1
        ).astype(BF)
        return carry

    lax.fori_loop(0, trows // ib, bias_body, 0)
    biases = [bias_copy(t2) for t2 in range(tiles)]
    for copy in biases:
        start(copy)

    def arrived(ref, sem):
        pltpu.make_async_copy(ref, ref, sem).wait()

    for t2 in range(tiles):
        arrived(left_ref.at[t2], recv_l.at[t2])
    for dt in range(1, tiles):
        src = lax.rem(t + dt, tiles)
        arrived(right_ref.at[src], recv_r.at[src])
    for dc in range(1, cols):
        src = lax.rem(c + dc, cols)
        arrived(normed_ref.at[src], recv_x.at[src])
    for k in range(n):
        for c2 in range(cols):
            arrived(bias_ref.at[k, c2], recv_b.at[k * cols + c2])
    for copy in lefts:
        finish(copy)
    for dt in range(1, tiles):
        right_copy(dt).wait_send()
    for dc in range(1, cols):
        normed_copy(dc).wait_send()
    for copy in biases:
        finish(copy)


def pair_kernel(
    depth,
    left_ref,
    right_ref,
    pair_ref,
    wp_ref,
    g_ref,
    widen_ref,
    shrink_ref,
    out_ref,
    rmat,
    wmat,
):
    tiles, prod, rows, tcols = right_ref.shape
    cz = pair_ref.shape[-1]
    pack = pair_ref.shape[0]

    @pl.when(pl.program_id(0) == 0)
    def _():
        for d in range(prod):
            for t in range(tiles):
                rmat[t * rows : (t + 1) * rows, d * tcols : (d + 1) * tcols] = right_ref[t, d]
        step = LANES // prod
        for d0 in range(0, prod, step):
            w = jnp.concatenate(
                [wp_ref[pl.ds(d, prod, stride=prod), :] for d in range(d0, d0 + step)], axis=0
            )
            wmat[:, d0 * prod : (d0 + step) * prod] = (w.T * (1.0 / depth)).astype(BF)

    left = jnp.concatenate([left_ref[t, 0] for t in range(tiles)], axis=0)
    left = left.astype(F32).T.astype(BF)
    dn = 8
    total = None
    for d0 in range(0, prod, dn):
        o = dot(left, rmat[:, d0 * tcols : (d0 + dn) * tcols]).astype(BF)
        cols = [
            jnp.concatenate(
                [
                    o[r * prod : (r + 1) * prod, d * tcols : (d + 1) * tcols]
                    for d in range(dn)
                ],
                axis=0,
            )
            for r in range(pack)
        ]
        part = dot(wmat[:, d0 * prod : (d0 + dn) * prod], jnp.concatenate(cols, axis=1))
        total = part if total is None else total + part
    mid = jnp.concatenate(
        [pair_ref[r] + total[:, r * tcols : (r + 1) * tcols].T for r in range(pack)], axis=0
    )
    h = (center(mid) * g_ref[...]).astype(BF)
    spread = jnp.maximum(dot(h, widen_ref[...]), 0.0).astype(BF)
    out = mid + dot(spread, shrink_ref[...])
    out_ref[...] = out.reshape(out_ref.shape)


def row_kernel(
    heads,
    normed_ref,
    bias_ref,
    x_ref,
    wq_ref,
    wk_ref,
    wv_ref,
    wo_ref,
    g_ref,
    widen_ref,
    shrink_ref,
    out_ref,
    bmat,
):
    cols, srows, res, feat = normed_ref.shape
    n, _, _, trows, tcols = bias_ref.shape
    dim = feat // heads
    me = lax.axis_index("col")

    @pl.when(pl.program_id(0) == 0)
    def _():
        for k in range(n):
            for c in range(cols):
                bmat[:, k * trows : (k + 1) * trows, c * tcols : (c + 1) * tcols] = (
                    bias_ref[k, c].astype(F32) * LOG2E
                )

    scale = LOG2E / dim**0.5
    lane = lax.broadcasted_iota(jnp.int32, (res, feat), 1) // dim
    mixed = []
    for s in range(srows):
        every = jnp.concatenate([normed_ref[c, s] for c in range(cols)], axis=0)
        q = dot(normed_ref[me, s], wq_ref[...]).astype(BF)
        key = dot(every, wk_ref[...]).astype(BF)
        value = dot(every, wv_ref[...]).astype(BF)
        acc = None
        for h in range(heads):
            qh = jnp.where(lane == h, q, jnp.zeros_like(q))
            logit = dot(qh, key, 1, 1) * scale + bmat[h]
            e = jnp.exp2(logit - jnp.max(logit, axis=-1, keepdims=True))
            w = (e * (1.0 / jnp.sum(e, axis=-1, keepdims=True))).astype(BF)
            o = dot(w, value)
            acc = o if acc is None else jnp.where(lane == h, o, acc)
        mixed.append(acc.astype(BF))
    mixed = jnp.concatenate(mixed, axis=0)
    mid = x_ref[...].reshape(srows * res, feat) + dot(mixed, wo_ref[...])
    y = (center(mid) * g_ref[...]).astype(BF)
    lifted = jnp.maximum(dot(y, widen_ref[...]), 0.0).astype(BF)
    out = mid + dot(lifted, shrink_ref[...])
    out_ref[...] = out.reshape(out_ref.shape)


def on_device(tiles, cols, *args):
    (x, pair, gm, gb, gf, gp, gg, bmap, wq, wk, wv, wo, widen, shrink, wl, wr, wp, gwiden, gshrink) = args
    _, rows, res, feat = x.shape
    _, trows, tcols, cz = pair.shape
    heads = bmap.shape[1]
    prod = wl.shape[1]
    aligned = (
        tiles % cols == 0
        and trows * (tiles // cols) == res
        and rows % 16 == 0
        and trows % 16 == 0
        and tcols % LANES == 0
        and res % LANES == 0
        and feat % LANES == 0
        and cz % LANES == 0
        and LANES % prod == 0
    )
    if not aligned:
        return plain_device(*args)
    n = tiles // cols
    pack = LANES // prod
    vm = pl.BlockSpec(memory_space=pltpu.VMEM)
    dma = pltpu.SemaphoreType.DMA
    sds = jax.ShapeDtypeStruct
    normed, left, right, bias = pl.pallas_call(
        functools.partial(exchange_kernel, tiles, cols),
        out_shape=(
            sds((cols, rows, res, feat), BF),
            sds((tiles, trows // pack, rows, LANES), BF),
            sds((tiles, prod, rows, tcols), BF),
            sds((n, cols, heads, trows, tcols), BF),
        ),
        in_specs=[vm] * 8,
        out_specs=(vm,) * 4,
        scratch_shapes=[
            pltpu.VMEM((feat // LANES, rows, res, LANES), F32),
            pltpu.VMEM((res // pack, rows, LANES), BF),
            pltpu.VMEM((heads, trows, tcols), BF),
            pltpu.VMEM((pack, LANES, feat), BF),
            dma((cols,)),
            dma((cols,)),
            dma((n * cols,)),
            dma((tiles,)),
            dma((tiles,)),
            dma((tiles,)),
            dma((tiles,)),
            dma((n * cols,)),
        ],
        compiler_params=pltpu.CompilerParams(
            collective_id=0, has_side_effects=True, vmem_limit_bytes=48 << 20
        ),
    )(x[0], pair[0], gm[None], gp[None], gb[None], bmap.T, wl.T, wr.T)

    def whole(a):
        return pl.BlockSpec(a.shape, lambda i: (0,) * a.ndim)

    gg2, gf2 = gg[None], gf[None]
    depth = rows * tiles
    grid_revised = pl.pallas_call(
        functools.partial(pair_kernel, depth),
        grid=(trows // pack,),
        out_shape=sds((trows, tcols, cz), F32),
        in_specs=[
            pl.BlockSpec((tiles, 1, rows, LANES), lambda i: (0, i, 0, 0)),
            whole(right),
            pl.BlockSpec((pack, tcols, cz), lambda i: (i, 0, 0)),
            whole(wp),
            whole(gg2),
            whole(gwiden),
            whole(gshrink),
        ],
        out_specs=pl.BlockSpec((pack, tcols, cz), lambda i: (i, 0, 0)),
        scratch_shapes=[
            pltpu.VMEM((depth, prod * tcols), BF),
            pltpu.VMEM((cz, prod * prod), BF),
        ],
        compiler_params=pltpu.CompilerParams(vmem_limit_bytes=48 << 20),
    )(left, right, pair[0], wp, gg2, gwiden, gshrink)

    srows = 2
    alignment_revised = pl.pallas_call(
        functools.partial(row_kernel, heads),
        grid=(rows // srows,),
        out_shape=sds((rows, res, feat), F32),
        in_specs=[
            pl.BlockSpec((cols, srows, res, feat), lambda i: (0, i, 0, 0)),
            whole(bias),
            pl.BlockSpec((srows, res, feat), lambda i: (i, 0, 0)),
            whole(wq),
            whole(wk),
            whole(wv),
            whole(wo),
            whole(gf2),
            whole(widen),
            whole(shrink),
        ],
        out_specs=pl.BlockSpec((srows, res, feat), lambda i: (i, 0, 0)),
        scratch_shapes=[pltpu.VMEM((heads, res, res * cols), F32)],
        compiler_params=pltpu.CompilerParams(vmem_limit_bytes=48 << 20),
    )(normed, bias, x[0], wq, wk, wv, wo, gf2, widen, shrink)
    return alignment_revised[None], grid_revised[None]


def solution(mesh):
    placed = (
        P(("groups", "branch"), "tile", "col", None),
        P(("groups", "branch"), "tile", "col", None),
        P(),
        P(),
        P(),
        P(),
        P(),
        P(),
        P(),
        P(),
        P(),
        P(),
        P(),
        P(),
        P(),
        P(),
        P(),
        P(),
        P(),
    )
    return jax.shard_map(
        functools.partial(on_device, mesh.shape["tile"], mesh.shape["col"]),
        mesh=mesh,
        in_specs=placed,
        out_specs=(
            P(("groups", "branch"), "tile", "col", None),
            P(("groups", "branch"), "tile", "col", None),
        ),
        check_vma=False,
    )
```

```python
import functools

import jax
import jax.numpy as jnp
from jax import lax
from jax.experimental import pallas as pl
from jax.experimental.pallas import tpu as pltpu
from jax.sharding import PartitionSpec as P

SEQUENCE_DEPTH = 64


def standardize_features(x, gain):
    mean = jnp.mean(x, axis=-1, keepdims=True)
    var = jnp.mean((x - mean) ** 2, axis=-1, keepdims=True)
    return (x - mean) * lax.rsqrt(var + 1e-05) * gain


def plain_device(
    alignment_tensor,
    residue_grid,
    mixing_scale_vector,
    logit_offset_scale,
    feedforward_scale,
    product_scale_vector,
    grid_scale_vector,
    logit_offset_map,
    asking_mapping,
    lookup_mapping,
    content_mapping,
    mixing_return_matrix,
    alignment_widen_map,
    alignment_shrink_map,
    former_embedding_map,
    latter_embedding_map,
    product_return_map,
    grid_widen_map,
    grid_shrink_map,
):
    sample_alignment = alignment_tensor[0]
    local_pair = residue_grid[0]
    subspace_total = logit_offset_map.shape[1]
    feature_extent = sample_alignment.shape[-1]
    subspace_number = feature_extent // subspace_total
    sequences_available = sample_alignment.shape[0]
    chain_available = sample_alignment.shape[1]
    tile_rows = local_pair.shape[0]
    tile_cols = local_pair.shape[1]
    product_extent = former_embedding_map.shape[1]
    product_operands = standardize_features(sample_alignment, product_scale_vector).astype(
        jnp.bfloat16
    )
    former_tensor = jnp.dot(
        product_operands, former_embedding_map, preferred_element_type=jnp.float32
    ).astype(jnp.bfloat16)
    latter_tensor = jnp.dot(
        product_operands, latter_embedding_map, preferred_element_type=jnp.float32
    ).astype(jnp.bfloat16)
    left_rows, right_rows = (
        lax.all_gather(former_tensor, "tile", axis=0, tiled=True),
        lax.all_gather(latter_tensor, "tile", axis=0, tiled=True),
    )
    left_all = lax.all_gather(left_rows, "col", axis=1, tiled=True)
    left_mine = lax.dynamic_slice_in_dim(left_all, lax.axis_index("tile") * tile_rows, tile_rows, 1)
    tensor_product = (
        jnp.einsum("era,eyq->ryaq", left_mine, right_rows, preferred_element_type=jnp.float32)
        / SEQUENCE_DEPTH
    )
    update = jnp.dot(
        tensor_product.reshape(tile_rows, tile_cols, product_extent * product_extent),
        product_return_map,
        precision=lax.Precision.HIGHEST,
    )
    bias_tile = jnp.einsum(
        "ijc,ch->hij",
        standardize_features(local_pair, logit_offset_scale),
        logit_offset_map,
        precision=lax.Precision.HIGHEST,
    )
    wide = lax.all_gather(bias_tile, "col", axis=2, tiled=True)
    whole = lax.all_gather(wide.astype(jnp.bfloat16), "tile", axis=1, tiled=True).astype(wide.dtype)
    bias = lax.dynamic_slice_in_dim(
        whole, lax.axis_index("col") * chain_available, chain_available, 1
    )
    standardized_source = standardize_features(sample_alignment, mixing_scale_vector).astype(
        jnp.bfloat16
    )
    asking_vectors = jnp.dot(
        standardized_source, asking_mapping, preferred_element_type=jnp.float32
    ).astype(jnp.bfloat16)
    lookup_vectors = jnp.dot(
        standardized_source, lookup_mapping, preferred_element_type=jnp.float32
    ).astype(jnp.bfloat16)
    content_vectors = jnp.dot(
        standardized_source, content_mapping, preferred_element_type=jnp.float32
    ).astype(jnp.bfloat16)
    all_keys, all_values = (
        lax.all_gather(lookup_vectors, "col", axis=1, tiled=True),
        lax.all_gather(content_vectors, "col", axis=1, tiled=True),
    )
    total_res = all_keys.shape[1]
    asking_vectors = asking_vectors.reshape(
        sequences_available, chain_available, subspace_total, subspace_number
    )
    all_keys = all_keys.reshape(sequences_available, total_res, subspace_total, subspace_number)
    all_values = all_values.reshape(sequences_available, total_res, subspace_total, subspace_number)
    scores = (
        jnp.einsum("sqhd,skhd->shqk", asking_vectors, all_keys, preferred_element_type=jnp.float32)
        / jnp.sqrt(jnp.float32(subspace_number))
        + bias[None]
    )
    weights = jax.nn.softmax(scores, axis=-1).astype(jnp.bfloat16)
    mixing_outcome = jnp.einsum(
        "shqk,skhd->sqhd", weights, all_values, preferred_element_type=jnp.float32
    )
    mixing_outcome = mixing_outcome.astype(jnp.bfloat16).reshape(
        sequences_available, chain_available, feature_extent
    )
    alignment_activations = sample_alignment + jnp.dot(
        mixing_outcome, mixing_return_matrix, preferred_element_type=jnp.float32
    )
    expanded_features = jax.nn.relu(
        jnp.dot(
            standardize_features(alignment_activations, feedforward_scale).astype(jnp.bfloat16),
            alignment_widen_map,
            preferred_element_type=jnp.float32,
        )
    ).astype(jnp.bfloat16)
    alignment_revised = alignment_activations + jnp.dot(
        expanded_features, alignment_shrink_map, preferred_element_type=jnp.float32
    )
    pair_mid = local_pair + update
    spread = jax.nn.relu(
        jnp.dot(
            standardize_features(pair_mid, grid_scale_vector).astype(jnp.bfloat16),
            grid_widen_map,
            preferred_element_type=jnp.float32,
        )
    ).astype(jnp.bfloat16)
    grid_revised = pair_mid + jnp.dot(spread, grid_shrink_map, preferred_element_type=jnp.float32)
    return (alignment_revised[None], grid_revised[None])


BF = jnp.bfloat16
F32 = jnp.float32
LANES = 128
LOG2E = 1.4426950408889634
MESH = pl.DeviceIdType.MESH


def center(x):
    mean = jnp.mean(x, axis=-1, keepdims=True)
    d = x - mean
    return d * lax.rsqrt(jnp.mean(d * d, axis=-1, keepdims=True) + 1e-05)


def dot(a, b, ca=1, cb=0):
    return lax.dot_general(a, b, (((ca,), (cb,)), ((), ())), preferred_element_type=F32)


def exchange_kernel(
    tiles,
    cols,
    x_ref,
    pair_ref,
    gm_ref,
    gp_ref,
    gb_ref,
    mapt_ref,
    wlt_ref,
    wrt_ref,
    wp_ref,
    g_ref,
    widen_ref,
    shrink_ref,
    normed_ref,
    left_ref,
    right_ref,
    bias_ref,
    out_ref,
    y_ref,
    lmine,
    bmine,
    wl4,
    rmat,
    wmat,
    send_x,
    recv_x,
    send_l,
    recv_l,
    send_r,
    recv_r,
    send_b,
    recv_b,
):
    t = lax.axis_index("tile")
    c = lax.axis_index("col")
    n = tiles // cols
    rows, res, feat = x_ref.shape
    trows, tcols, cz = pair_ref.shape
    prod = wlt_ref.shape[0]
    pack = LANES // prod
    barrier = pltpu.get_barrier_semaphore()
    for dt in range(tiles):
        for dc in range(cols):
            if dt or dc:
                pl.semaphore_signal(
                    barrier,
                    inc=1,
                    device_id={
                        "tile": lax.rem(t + dt, tiles),
                        "col": lax.rem(c + dc, cols),
                    },
                    device_id_type=MESH,
                )

    wlt = wlt_ref[...]
    wl4[...] = jnp.zeros_like(wl4)
    for r in range(pack):
        wl4[r, r * prod : (r + 1) * prod, :] = wlt
    gp = gp_ref[...]
    gm = gm_ref[...]
    own = normed_ref.at[c]
    chunks = feat // LANES

    def factor(w, s, at):
        parts = [y_ref[(f, s) + at].astype(BF) for f in range(chunks)]
        return dot(w, jnp.concatenate(parts, axis=1), 1, 1)

    def rows_body(s, carry):
        z = center(x_ref[s])
        y = z * gp
        for f in range(chunks):
            y_ref[f, s, :, :] = y[:, f * LANES : (f + 1) * LANES]
        own[s, :, :] = (z * gm).astype(BF)
        return carry

    lax.fori_loop(0, rows, rows_body, 0)

    group = 16
    for s0 in range(0, rows, group):
        right = jnp.stack(
            [factor(wrt_ref[...], s, ()) for s in range(s0, s0 + group)]
        )
        right_ref[t, :, s0 : s0 + group, :] = jnp.swapaxes(right, 0, 1).astype(BF)
        left = []
        for s in range(s0, s0 + group):
            acc = None
            for r in range(pack):
                at = (pl.ds(r, res // pack, stride=pack), slice(None))
                parts = [y_ref[(f, s) + at].astype(BF) for f in range(chunks)]
                part = dot(jnp.concatenate(parts, axis=1), wl4[r], 1, 1)
                acc = part if acc is None else acc + part
            left.append(acc)
        lmine[:, s0 : s0 + group, :] = jnp.swapaxes(jnp.stack(left), 0, 1).astype(BF)

    pl.semaphore_wait(barrier, tiles * cols - 1)

    piece = trows // pack

    def left_copy(k, c2):
        dest = c * n + k
        src = lmine.at[pl.ds(k * piece, piece)]
        i = k * cols + c2
        away = jnp.logical_or(dest != t, c != c2)
        remote = pltpu.make_async_remote_copy(
            src_ref=src,
            dst_ref=left_ref.at[t],
            send_sem=send_l.at[i],
            recv_sem=recv_l.at[t],
            device_id={"tile": dest, "col": c2},
            device_id_type=MESH,
        )
        local = pltpu.make_async_copy(src, left_ref.at[t], recv_l.at[t])
        return away, remote, local

    def bias_copy(t2):
        owner = t // n
        slot = bias_ref.at[lax.rem(t, n), c]
        sem = recv_b.at[lax.rem(t, n) * cols + c]
        away = jnp.logical_or(t2 != t, c != owner)
        remote = pltpu.make_async_remote_copy(
            src_ref=bmine,
            dst_ref=slot,
            send_sem=send_b.at[t2],
            recv_sem=sem,
            device_id={"tile": t2, "col": owner},
            device_id_type=MESH,
        )
        local = pltpu.make_async_copy(bmine, slot, sem)
        return away, remote, local

    def start(copy):
        away, remote, local = copy

        @pl.when(away)
        def _():
            remote.start()

        @pl.when(jnp.logical_not(away))
        def _():
            local.start()

    def finish(copy):
        away, remote, _ = copy

        @pl.when(away)
        def _():
            remote.wait_send()

    def right_copy(dt):
        return pltpu.make_async_remote_copy(
            src_ref=right_ref.at[t],
            dst_ref=right_ref.at[t],
            send_sem=send_r.at[dt],
            recv_sem=recv_r.at[t],
            device_id={"tile": lax.rem(t + dt, tiles)},
            device_id_type=MESH,
        )

    def normed_copy(dc):
        return pltpu.make_async_remote_copy(
            src_ref=own,
            dst_ref=own,
            send_sem=send_x.at[dc],
            recv_sem=recv_x.at[c],
            device_id={"col": lax.rem(c + dc, cols)},
            device_id_type=MESH,
        )

    lefts = [left_copy(k, c2) for k in range(n) for c2 in range(cols)]
    for copy in lefts:
        start(copy)
    for dt in range(1, tiles):
        right_copy(dt).start()
    for dc in range(1, cols):
        normed_copy(dc).start()

    mapt = mapt_ref[...] * gb_ref[...]
    high = mapt.astype(BF)
    low = (mapt - high.astype(F32)).astype(BF)
    both = jnp.concatenate([high.astype(F32), low.astype(F32)], axis=0).astype(BF)
    heads = mapt.shape[0]
    ib = 16

    def bias_body(b, carry):
        z = center(pair_ref[pl.ds(b * ib, ib)]).astype(BF)
        out = []
        for i in range(ib):
            p = dot(both, z[i], 1, 1)
            out.append(p[:heads] + p[heads:])
        bmine[:, pl.ds(pl.multiple_of(b * ib, ib), ib), :] = jnp.swapaxes(
            jnp.stack(out), 0, 1
        ).astype(BF)
        return carry

    lax.fori_loop(0, trows // ib, bias_body, 0)
    reorder(rows * tiles, prod, wp_ref, wmat)
    biases = [bias_copy(t2) for t2 in range(tiles)]
    for copy in biases:
        start(copy)

    def arrived(ref, sem):
        pltpu.make_async_copy(ref, ref, sem).wait()

    for t2 in range(tiles):
        arrived(left_ref.at[t2], recv_l.at[t2])
    for dt in range(1, tiles):
        src = lax.rem(t + dt, tiles)
        arrived(right_ref.at[src], recv_r.at[src])

    widen_right(right_ref, rmat)

    def pair_body(m, carry):
        pair_step(m, pack, left_ref, pair_ref, g_ref, widen_ref, shrink_ref, out_ref, rmat, wmat)
        return carry

    lax.fori_loop(0, trows // pack, pair_body, 0)

    for dc in range(1, cols):
        src = lax.rem(c + dc, cols)
        arrived(normed_ref.at[src], recv_x.at[src])
    for k in range(n):
        for c2 in range(cols):
            arrived(bias_ref.at[k, c2], recv_b.at[k * cols + c2])
    for copy in lefts:
        finish(copy)
    for dt in range(1, tiles):
        right_copy(dt).wait_send()
    for dc in range(1, cols):
        normed_copy(dc).wait_send()
    for copy in biases:
        finish(copy)


def widen_right(right_ref, rmat):
    tiles, prod, rows, tcols = right_ref.shape
    for d in range(prod):
        for t in range(tiles):
            rmat[t * rows : (t + 1) * rows, d * tcols : (d + 1) * tcols] = right_ref[t, d]


def reorder(depth, prod, wp_ref, wmat):
    step = LANES // prod
    for d0 in range(0, prod, step):
        w = jnp.concatenate(
            [wp_ref[pl.ds(d, prod, stride=prod), :] for d in range(d0, d0 + step)], axis=0
        )
        wmat[:, d0 * prod : (d0 + step) * prod] = (w.T * (1.0 / depth)).astype(BF)


def pair_step(m, pack, left_ref, pair_ref, g_ref, widen_ref, shrink_ref, out_ref, rmat, wmat):
    tiles = left_ref.shape[0]
    _, tcols, cz = pair_ref.shape
    prod = LANES // pack
    left = jnp.concatenate([left_ref[t, m] for t in range(tiles)], axis=0)
    left = left.astype(F32).T.astype(BF)
    dn = 8
    total = None
    for d0 in range(0, prod, dn):
        o = dot(left, rmat[:, d0 * tcols : (d0 + dn) * tcols]).astype(BF)
        cols = [
            jnp.concatenate(
                [
                    o[r * prod : (r + 1) * prod, d * tcols : (d + 1) * tcols]
                    for d in range(dn)
                ],
                axis=0,
            )
            for r in range(pack)
        ]
        part = dot(wmat[:, d0 * prod : (d0 + dn) * prod], jnp.concatenate(cols, axis=1))
        total = part if total is None else total + part
    mid = jnp.concatenate(
        [pair_ref[m * pack + r] + total[:, r * tcols : (r + 1) * tcols].T for r in range(pack)],
        axis=0,
    )
    h = (center(mid) * g_ref[...]).astype(BF)
    spread = jnp.maximum(dot(h, widen_ref[...]), 0.0).astype(BF)
    out = mid + dot(spread, shrink_ref[...])
    out_ref[pl.ds(m * pack, pack)] = out.reshape(pack, tcols, cz)


def row_kernel(
    heads,
    normed_ref,
    bias_ref,
    x_ref,
    wq_ref,
    wk_ref,
    wv_ref,
    wo_ref,
    g_ref,
    widen_ref,
    shrink_ref,
    out_ref,
    bmat,
):
    cols, srows, res, feat = normed_ref.shape
    n, _, _, trows, tcols = bias_ref.shape
    dim = feat // heads
    me = lax.axis_index("col")

    @pl.when(pl.program_id(0) == 0)
    def _():
        for k in range(n):
            for c in range(cols):
                for h in range(heads):
                    row = h * res + k * trows
                    bmat[row : row + trows, c * tcols : (c + 1) * tcols] = (
                        bias_ref[k, c, h].astype(F32) * LOG2E
                    )

    scale = LOG2E / dim**0.5
    lane = lax.broadcasted_iota(jnp.int32, (res, feat), 1) // dim
    some = LANES // dim
    local = lax.broadcasted_iota(jnp.int32, (res, LANES), 1) // dim
    ones = jnp.ones((res * cols, LANES), BF)
    mixed = []
    for s in range(srows):
        every = jnp.concatenate([normed_ref[c, s] for c in range(cols)], axis=0)
        q = dot(normed_ref[me, s], wq_ref[...]).astype(BF)
        key = dot(every, wk_ref[...]).astype(BF)
        value = dot(every, wv_ref[...]).astype(BF)
        groups = []
        for h0 in range(0, heads, some):
            qs = jnp.concatenate(
                [jnp.where(lane == h, q, jnp.zeros_like(q)) for h in range(h0, h0 + some)], axis=0
            )
            logit = dot(qs, key, 1, 1) * scale + bmat[h0 * res : (h0 + some) * res, :]
            e = jnp.exp2(logit - jnp.max(logit, axis=-1, keepdims=True)).astype(BF)
            o = dot(e, jnp.concatenate([value[:, h0 * dim : (h0 + some) * dim], ones], axis=1))
            top = o[:res, :LANES]
            low = o[:res, LANES:]
            for k in range(1, some):
                top = jnp.where(local == k, o[k * res : (k + 1) * res, :LANES], top)
                low = jnp.where(local == k, o[k * res : (k + 1) * res, LANES:], low)
            groups.append((top / low).astype(BF))
        mixed.append(jnp.concatenate(groups, axis=1))
    mixed = jnp.concatenate(mixed, axis=0)
    mid = x_ref[...].reshape(srows * res, feat) + dot(mixed, wo_ref[...])
    y = (center(mid) * g_ref[...]).astype(BF)
    lifted = jnp.maximum(dot(y, widen_ref[...]), 0.0).astype(BF)
    out = mid + dot(lifted, shrink_ref[...])
    out_ref[...] = out.reshape(out_ref.shape)


def on_device(tiles, cols, *args):
    (x, pair, gm, gb, gf, gp, gg, bmap, wq, wk, wv, wo, widen, shrink, wl, wr, wp, gwiden, gshrink) = args
    _, rows, res, feat = x.shape
    _, trows, tcols, cz = pair.shape
    heads = bmap.shape[1]
    prod = wl.shape[1]
    aligned = (
        tiles % cols == 0
        and trows * (tiles // cols) == res
        and rows % 16 == 0
        and trows % 16 == 0
        and tcols % LANES == 0
        and res % LANES == 0
        and feat % LANES == 0
        and cz % LANES == 0
        and LANES % prod == 0
        and LANES % (feat // heads) == 0
        and rows % 2 == 0
    )
    if not aligned:
        return plain_device(*args)
    n = tiles // cols
    pack = LANES // prod
    vm = pl.BlockSpec(memory_space=pltpu.VMEM)
    dma = pltpu.SemaphoreType.DMA
    sds = jax.ShapeDtypeStruct
    normed, left, right, bias, grid_revised = pl.pallas_call(
        functools.partial(exchange_kernel, tiles, cols),
        out_shape=(
            sds((cols, rows, res, feat), BF),
            sds((tiles, trows // pack, rows, LANES), BF),
            sds((tiles, prod, rows, tcols), BF),
            sds((n, cols, heads, trows, tcols), BF),
            sds((trows, tcols, cz), F32),
        ),
        in_specs=[vm] * 12,
        out_specs=(vm,) * 5,
        scratch_shapes=[
            pltpu.VMEM((feat // LANES, rows, res, LANES), F32),
            pltpu.VMEM((res // pack, rows, LANES), BF),
            pltpu.VMEM((heads, trows, tcols), BF),
            pltpu.VMEM((pack, LANES, feat), BF),
            pltpu.VMEM((rows * tiles, prod * tcols), BF),
            pltpu.VMEM((cz, prod * prod), BF),
            dma((cols,)),
            dma((cols,)),
            dma((n * cols,)),
            dma((tiles,)),
            dma((tiles,)),
            dma((tiles,)),
            dma((tiles,)),
            dma((n * cols,)),
        ],
        compiler_params=pltpu.CompilerParams(
            collective_id=0, has_side_effects=True, vmem_limit_bytes=48 << 20
        ),
    )(x[0], pair[0], gm[None], gp[None], gb[None], bmap.T, wl.T, wr.T, wp, gg[None], gwiden, gshrink)

    def whole(a):
        return pl.BlockSpec(a.shape, lambda i: (0,) * a.ndim)

    gf2 = gf[None]
    srows = 2
    alignment_revised = pl.pallas_call(
        functools.partial(row_kernel, heads),
        grid=(rows // srows,),
        out_shape=sds((rows, res, feat), F32),
        in_specs=[
            pl.BlockSpec((cols, srows, res, feat), lambda i: (0, i, 0, 0)),
            whole(bias),
            pl.BlockSpec((srows, res, feat), lambda i: (i, 0, 0)),
            whole(wq),
            whole(wk),
            whole(wv),
            whole(wo),
            whole(gf2),
            whole(widen),
            whole(shrink),
        ],
        out_specs=pl.BlockSpec((srows, res, feat), lambda i: (i, 0, 0)),
        scratch_shapes=[pltpu.VMEM((heads * res, res * cols), F32)],
        compiler_params=pltpu.CompilerParams(vmem_limit_bytes=48 << 20),
    )(normed, bias, x[0], wq, wk, wv, wo, gf2, widen, shrink)
    return alignment_revised[None], grid_revised[None]


def solution(mesh):
    placed = (
        P(("groups", "branch"), "tile", "col", None),
        P(("groups", "branch"), "tile", "col", None),
        P(),
        P(),
        P(),
        P(),
        P(),
        P(),
        P(),
        P(),
        P(),
        P(),
        P(),
        P(),
        P(),
        P(),
        P(),
        P(),
        P(),
    )
    return jax.shard_map(
        functools.partial(on_device, mesh.shape["tile"], mesh.shape["col"]),
        mesh=mesh,
        in_specs=placed,
        out_specs=(
            P(("groups", "branch"), "tile", "col", None),
            P(("groups", "branch"), "tile", "col", None),
        ),
        check_vma=False,
    )
```

```python
import functools

import jax
import jax.numpy as jnp
from jax import lax
from jax.experimental import pallas as pl
from jax.experimental.pallas import tpu as pltpu
from jax.sharding import PartitionSpec as P

SEQUENCE_DEPTH = 64


def standardize_features(x, gain):
    mean = jnp.mean(x, axis=-1, keepdims=True)
    var = jnp.mean((x - mean) ** 2, axis=-1, keepdims=True)
    return (x - mean) * lax.rsqrt(var + 1e-05) * gain


def plain_device(
    alignment_tensor,
    residue_grid,
    mixing_scale_vector,
    logit_offset_scale,
    feedforward_scale,
    product_scale_vector,
    grid_scale_vector,
    logit_offset_map,
    asking_mapping,
    lookup_mapping,
    content_mapping,
    mixing_return_matrix,
    alignment_widen_map,
    alignment_shrink_map,
    former_embedding_map,
    latter_embedding_map,
    product_return_map,
    grid_widen_map,
    grid_shrink_map,
):
    sample_alignment = alignment_tensor[0]
    local_pair = residue_grid[0]
    subspace_total = logit_offset_map.shape[1]
    feature_extent = sample_alignment.shape[-1]
    subspace_number = feature_extent // subspace_total
    sequences_available = sample_alignment.shape[0]
    chain_available = sample_alignment.shape[1]
    tile_rows = local_pair.shape[0]
    tile_cols = local_pair.shape[1]
    product_extent = former_embedding_map.shape[1]
    product_operands = standardize_features(sample_alignment, product_scale_vector).astype(
        jnp.bfloat16
    )
    former_tensor = jnp.dot(
        product_operands, former_embedding_map, preferred_element_type=jnp.float32
    ).astype(jnp.bfloat16)
    latter_tensor = jnp.dot(
        product_operands, latter_embedding_map, preferred_element_type=jnp.float32
    ).astype(jnp.bfloat16)
    left_rows, right_rows = (
        lax.all_gather(former_tensor, "tile", axis=0, tiled=True),
        lax.all_gather(latter_tensor, "tile", axis=0, tiled=True),
    )
    left_all = lax.all_gather(left_rows, "col", axis=1, tiled=True)
    left_mine = lax.dynamic_slice_in_dim(left_all, lax.axis_index("tile") * tile_rows, tile_rows, 1)
    tensor_product = (
        jnp.einsum("era,eyq->ryaq", left_mine, right_rows, preferred_element_type=jnp.float32)
        / SEQUENCE_DEPTH
    )
    update = jnp.dot(
        tensor_product.reshape(tile_rows, tile_cols, product_extent * product_extent),
        product_return_map,
        precision=lax.Precision.HIGHEST,
    )
    bias_tile = jnp.einsum(
        "ijc,ch->hij",
        standardize_features(local_pair, logit_offset_scale),
        logit_offset_map,
        precision=lax.Precision.HIGHEST,
    )
    wide = lax.all_gather(bias_tile, "col", axis=2, tiled=True)
    whole = lax.all_gather(wide.astype(jnp.bfloat16), "tile", axis=1, tiled=True).astype(wide.dtype)
    bias = lax.dynamic_slice_in_dim(
        whole, lax.axis_index("col") * chain_available, chain_available, 1
    )
    standardized_source = standardize_features(sample_alignment, mixing_scale_vector).astype(
        jnp.bfloat16
    )
    asking_vectors = jnp.dot(
        standardized_source, asking_mapping, preferred_element_type=jnp.float32
    ).astype(jnp.bfloat16)
    lookup_vectors = jnp.dot(
        standardized_source, lookup_mapping, preferred_element_type=jnp.float32
    ).astype(jnp.bfloat16)
    content_vectors = jnp.dot(
        standardized_source, content_mapping, preferred_element_type=jnp.float32
    ).astype(jnp.bfloat16)
    all_keys, all_values = (
        lax.all_gather(lookup_vectors, "col", axis=1, tiled=True),
        lax.all_gather(content_vectors, "col", axis=1, tiled=True),
    )
    total_res = all_keys.shape[1]
    asking_vectors = asking_vectors.reshape(
        sequences_available, chain_available, subspace_total, subspace_number
    )
    all_keys = all_keys.reshape(sequences_available, total_res, subspace_total, subspace_number)
    all_values = all_values.reshape(sequences_available, total_res, subspace_total, subspace_number)
    scores = (
        jnp.einsum("sqhd,skhd->shqk", asking_vectors, all_keys, preferred_element_type=jnp.float32)
        / jnp.sqrt(jnp.float32(subspace_number))
        + bias[None]
    )
    weights = jax.nn.softmax(scores, axis=-1).astype(jnp.bfloat16)
    mixing_outcome = jnp.einsum(
        "shqk,skhd->sqhd", weights, all_values, preferred_element_type=jnp.float32
    )
    mixing_outcome = mixing_outcome.astype(jnp.bfloat16).reshape(
        sequences_available, chain_available, feature_extent
    )
    alignment_activations = sample_alignment + jnp.dot(
        mixing_outcome, mixing_return_matrix, preferred_element_type=jnp.float32
    )
    expanded_features = jax.nn.relu(
        jnp.dot(
            standardize_features(alignment_activations, feedforward_scale).astype(jnp.bfloat16),
            alignment_widen_map,
            preferred_element_type=jnp.float32,
        )
    ).astype(jnp.bfloat16)
    alignment_revised = alignment_activations + jnp.dot(
        expanded_features, alignment_shrink_map, preferred_element_type=jnp.float32
    )
    pair_mid = local_pair + update
    spread = jax.nn.relu(
        jnp.dot(
            standardize_features(pair_mid, grid_scale_vector).astype(jnp.bfloat16),
            grid_widen_map,
            preferred_element_type=jnp.float32,
        )
    ).astype(jnp.bfloat16)
    grid_revised = pair_mid + jnp.dot(spread, grid_shrink_map, preferred_element_type=jnp.float32)
    return (alignment_revised[None], grid_revised[None])


BF = jnp.bfloat16
F32 = jnp.float32
LANES = 128
LOG2E = 1.4426950408889634
MESH = pl.DeviceIdType.MESH


def center(x):
    mean = jnp.mean(x, axis=-1, keepdims=True)
    d = x - mean
    return d * lax.rsqrt(jnp.mean(d * d, axis=-1, keepdims=True) + 1e-05)


def dot(a, b, ca=1, cb=0):
    return lax.dot_general(a, b, (((ca,), (cb,)), ((), ())), preferred_element_type=F32)


def exchange_kernel(
    tiles,
    cols,
    x_ref,
    pair_ref,
    gm_ref,
    gp_ref,
    gb_ref,
    mapt_ref,
    wlt_ref,
    wrt_ref,
    wp_ref,
    g_ref,
    widen_ref,
    shrink_ref,
    normed_ref,
    left_ref,
    right_ref,
    bias_ref,
    out_ref,
    y_ref,
    lmine,
    bmine,
    wl4,
    rmat,
    wmat,
    send_x,
    recv_x,
    send_l,
    recv_l,
    send_r,
    recv_r,
    send_b,
    recv_b,
):
    t = lax.axis_index("tile")
    c = lax.axis_index("col")
    n = tiles // cols
    rows, res, feat = x_ref.shape
    trows, tcols, cz = pair_ref.shape
    prod = wlt_ref.shape[0]
    pack = LANES // prod
    barrier = pltpu.get_barrier_semaphore()
    for dt in range(tiles):
        for dc in range(cols):
            if dt or dc:
                pl.semaphore_signal(
                    barrier,
                    inc=1,
                    device_id={
                        "tile": lax.rem(t + dt, tiles),
                        "col": lax.rem(c + dc, cols),
                    },
                    device_id_type=MESH,
                )

    wlt = wlt_ref[...]
    wl4[...] = jnp.zeros_like(wl4)
    for r in range(pack):
        wl4[r, r * prod : (r + 1) * prod, :] = wlt
    gp = gp_ref[...]
    gm = gm_ref[...]
    own = normed_ref.at[c]
    chunks = feat // LANES

    def factor(w, s, at):
        parts = [y_ref[(f, s) + at].astype(BF) for f in range(chunks)]
        return dot(w, jnp.concatenate(parts, axis=1), 1, 1)

    def rows_body(s, carry):
        z = center(x_ref[s])
        y = z * gp
        for f in range(chunks):
            y_ref[f, s, :, :] = y[:, f * LANES : (f + 1) * LANES]
        own[s, :, :] = (z * gm).astype(BF)
        return carry

    lax.fori_loop(0, rows, rows_body, 0, unroll=2)

    group = 16
    for s0 in range(0, rows, group):
        right = jnp.stack(
            [factor(wrt_ref[...], s, ()) for s in range(s0, s0 + group)]
        )
        right_ref[t, :, s0 : s0 + group, :] = jnp.swapaxes(right, 0, 1).astype(BF)
        left = []
        for s in range(s0, s0 + group):
            acc = None
            for r in range(pack):
                at = (pl.ds(r, res // pack, stride=pack), slice(None))
                parts = [y_ref[(f, s) + at].astype(BF) for f in range(chunks)]
                part = dot(jnp.concatenate(parts, axis=1), wl4[r], 1, 1)
                acc = part if acc is None else acc + part
            left.append(acc)
        lmine[:, s0 : s0 + group, :] = jnp.swapaxes(jnp.stack(left), 0, 1).astype(BF)

    pl.semaphore_wait(barrier, tiles * cols - 1)

    piece = trows // pack

    def left_copy(k, c2):
        dest = c * n + k
        src = lmine.at[pl.ds(k * piece, piece)]
        i = k * cols + c2
        away = jnp.logical_or(dest != t, c != c2)
        remote = pltpu.make_async_remote_copy(
            src_ref=src,
            dst_ref=left_ref.at[t],
            send_sem=send_l.at[i],
            recv_sem=recv_l.at[t],
            device_id={"tile": dest, "col": c2},
            device_id_type=MESH,
        )
        local = pltpu.make_async_copy(src, left_ref.at[t], recv_l.at[t])
        return away, remote, local

    def bias_copy(t2):
        owner = t // n
        slot = bias_ref.at[lax.rem(t, n), c]
        sem = recv_b.at[lax.rem(t, n) * cols + c]
        away = jnp.logical_or(t2 != t, c != owner)
        remote = pltpu.make_async_remote_copy(
            src_ref=bmine,
            dst_ref=slot,
            send_sem=send_b.at[t2],
            recv_sem=sem,
            device_id={"tile": t2, "col": owner},
            device_id_type=MESH,
        )
        local = pltpu.make_async_copy(bmine, slot, sem)
        return away, remote, local

    def start(copy):
        away, remote, local = copy

        @pl.when(away)
        def _():
            remote.start()

        @pl.when(jnp.logical_not(away))
        def _():
            local.start()

    def finish(copy):
        away, remote, _ = copy

        @pl.when(away)
        def _():
            remote.wait_send()

    def right_copy(dt):
        return pltpu.make_async_remote_copy(
            src_ref=right_ref.at[t],
            dst_ref=right_ref.at[t],
            send_sem=send_r.at[dt],
            recv_sem=recv_r.at[t],
            device_id={"tile": lax.rem(t + dt, tiles)},
            device_id_type=MESH,
        )

    def normed_copy(dc):
        return pltpu.make_async_remote_copy(
            src_ref=own,
            dst_ref=own,
            send_sem=send_x.at[dc],
            recv_sem=recv_x.at[c],
            device_id={"col": lax.rem(c + dc, cols)},
            device_id_type=MESH,
        )

    lefts = [left_copy(k, c2) for k in range(n) for c2 in range(cols)]
    for copy in lefts:
        start(copy)
    for dt in range(1, tiles):
        right_copy(dt).start()

    mapt = mapt_ref[...] * gb_ref[...]
    high = mapt.astype(BF)
    low = (mapt - high.astype(F32)).astype(BF)
    both = jnp.concatenate([high.astype(F32), low.astype(F32)], axis=0).astype(BF)
    heads = mapt.shape[0]
    ib = 16

    def bias_body(b, carry):
        z = center(pair_ref[pl.ds(b * ib, ib)]).astype(BF)
        out = []
        for i in range(ib):
            p = dot(both, z[i], 1, 1)
            out.append(p[:heads] + p[heads:])
        bmine[:, pl.ds(pl.multiple_of(b * ib, ib), ib), :] = jnp.swapaxes(
            jnp.stack(out), 0, 1
        ).astype(BF)
        return carry

    lax.fori_loop(0, trows // ib, bias_body, 0)
    reorder(rows * tiles, prod, wp_ref, wmat)
    biases = [bias_copy(t2) for t2 in range(tiles)]
    def arrived(ref, sem):
        pltpu.make_async_copy(ref, ref, sem).wait()

    for t2 in range(tiles):
        arrived(left_ref.at[t2], recv_l.at[t2])
    for dt in range(1, tiles):
        src = lax.rem(t + dt, tiles)
        arrived(right_ref.at[src], recv_r.at[src])
    for copy in biases:
        start(copy)
    for dc in range(1, cols):
        normed_copy(dc).start()

    widen_right(right_ref, rmat)

    def pair_body(m, carry):
        pair_step(m, pack, left_ref, pair_ref, g_ref, widen_ref, shrink_ref, out_ref, rmat, wmat)
        return carry

    lax.fori_loop(0, trows // pack, pair_body, 0, unroll=2)

    for dc in range(1, cols):
        src = lax.rem(c + dc, cols)
        arrived(normed_ref.at[src], recv_x.at[src])
    for k in range(n):
        for c2 in range(cols):
            arrived(bias_ref.at[k, c2], recv_b.at[k * cols + c2])
    for copy in lefts:
        finish(copy)
    for dt in range(1, tiles):
        right_copy(dt).wait_send()
    for dc in range(1, cols):
        normed_copy(dc).wait_send()
    for copy in biases:
        finish(copy)


def widen_right(right_ref, rmat):
    tiles, prod, rows, tcols = right_ref.shape
    for d in range(prod):
        for t in range(tiles):
            rmat[t * rows : (t + 1) * rows, d * tcols : (d + 1) * tcols] = right_ref[t, d]


def reorder(depth, prod, wp_ref, wmat):
    step = LANES // prod
    for d0 in range(0, prod, step):
        w = jnp.concatenate(
            [wp_ref[pl.ds(d, prod, stride=prod), :] for d in range(d0, d0 + step)], axis=0
        )
        wmat[:, d0 * prod : (d0 + step) * prod] = (w.T * (1.0 / depth)).astype(BF)


def pair_step(m, pack, left_ref, pair_ref, g_ref, widen_ref, shrink_ref, out_ref, rmat, wmat):
    tiles = left_ref.shape[0]
    _, tcols, cz = pair_ref.shape
    prod = LANES // pack
    left = jnp.concatenate([left_ref[t, m] for t in range(tiles)], axis=0)
    left = left.astype(F32).T.astype(BF)
    dn = 8
    total = None
    for d0 in range(0, prod, dn):
        o = dot(left, rmat[:, d0 * tcols : (d0 + dn) * tcols]).astype(BF)
        cols = [
            jnp.concatenate(
                [
                    o[r * prod : (r + 1) * prod, d * tcols : (d + 1) * tcols]
                    for d in range(dn)
                ],
                axis=0,
            )
            for r in range(pack)
        ]
        part = dot(wmat[:, d0 * prod : (d0 + dn) * prod], jnp.concatenate(cols, axis=1))
        total = part if total is None else total + part
    mid = jnp.concatenate(
        [pair_ref[m * pack + r] + total[:, r * tcols : (r + 1) * tcols].T for r in range(pack)],
        axis=0,
    )
    h = (center(mid) * g_ref[...]).astype(BF)
    spread = jnp.maximum(dot(h, widen_ref[...]), 0.0).astype(BF)
    out = mid + dot(spread, shrink_ref[...])
    out_ref[pl.ds(m * pack, pack)] = out.reshape(pack, tcols, cz)


def row_kernel(
    heads,
    normed_ref,
    bias_ref,
    x_ref,
    wq_ref,
    wk_ref,
    wv_ref,
    wo_ref,
    g_ref,
    widen_ref,
    shrink_ref,
    out_ref,
    bmat,
):
    cols, srows, res, feat = normed_ref.shape
    n, _, _, trows, tcols = bias_ref.shape
    dim = feat // heads
    me = lax.axis_index("col")

    @pl.when(pl.program_id(0) == 0)
    def _():
        for k in range(n):
            for c in range(cols):
                for h in range(heads):
                    row = h * res + k * trows
                    bmat[row : row + trows, c * tcols : (c + 1) * tcols] = (
                        bias_ref[k, c, h].astype(F32) * LOG2E
                    )

    scale = LOG2E / dim**0.5
    lane = lax.broadcasted_iota(jnp.int32, (res, feat), 1) // dim
    some = LANES // dim
    local = lax.broadcasted_iota(jnp.int32, (res, LANES), 1) // dim
    ones = jnp.ones((res * cols, LANES), BF)
    mixed = []
    for s in range(srows):
        every = jnp.concatenate([normed_ref[c, s] for c in range(cols)], axis=0)
        q = dot(normed_ref[me, s], wq_ref[...]).astype(BF)
        key = dot(every, wk_ref[...]).astype(BF)
        value = dot(every, wv_ref[...]).astype(BF)
        groups = []
        for h0 in range(0, heads, some):
            qs = jnp.concatenate(
                [jnp.where(lane == h, q, jnp.zeros_like(q)) for h in range(h0, h0 + some)], axis=0
            )
            logit = dot(qs, key, 1, 1) * scale + bmat[h0 * res : (h0 + some) * res, :]
            e = jnp.exp2(logit - jnp.max(logit, axis=-1, keepdims=True)).astype(BF)
            o = dot(e, jnp.concatenate([value[:, h0 * dim : (h0 + some) * dim], ones], axis=1))
            top = o[:res, :LANES]
            low = o[:res, LANES:]
            for k in range(1, some):
                top = jnp.where(local == k, o[k * res : (k + 1) * res, :LANES], top)
                low = jnp.where(local == k, o[k * res : (k + 1) * res, LANES:], low)
            groups.append((top / low).astype(BF))
        mixed.append(jnp.concatenate(groups, axis=1))
    mixed = jnp.concatenate(mixed, axis=0)
    mid = x_ref[...].reshape(srows * res, feat) + dot(mixed, wo_ref[...])
    y = (center(mid) * g_ref[...]).astype(BF)
    lifted = jnp.maximum(dot(y, widen_ref[...]), 0.0).astype(BF)
    out = mid + dot(lifted, shrink_ref[...])
    out_ref[...] = out.reshape(out_ref.shape)


def on_device(tiles, cols, *args):
    (x, pair, gm, gb, gf, gp, gg, bmap, wq, wk, wv, wo, widen, shrink, wl, wr, wp, gwiden, gshrink) = args
    _, rows, res, feat = x.shape
    _, trows, tcols, cz = pair.shape
    heads = bmap.shape[1]
    prod = wl.shape[1]
    aligned = (
        tiles % cols == 0
        and trows * (tiles // cols) == res
        and rows % 16 == 0
        and trows % 16 == 0
        and tcols % LANES == 0
        and res % LANES == 0
        and feat % LANES == 0
        and cz % LANES == 0
        and LANES % prod == 0
        and LANES % (feat // heads) == 0
        and rows % 2 == 0
    )
    if not aligned:
        return plain_device(*args)
    n = tiles // cols
    pack = LANES // prod
    vm = pl.BlockSpec(memory_space=pltpu.VMEM)
    dma = pltpu.SemaphoreType.DMA
    sds = jax.ShapeDtypeStruct
    normed, left, right, bias, grid_revised = pl.pallas_call(
        functools.partial(exchange_kernel, tiles, cols),
        out_shape=(
            sds((cols, rows, res, feat), BF),
            sds((tiles, trows // pack, rows, LANES), BF),
            sds((tiles, prod, rows, tcols), BF),
            sds((n, cols, heads, trows, tcols), BF),
            sds((trows, tcols, cz), F32),
        ),
        in_specs=[vm] * 12,
        out_specs=(vm,) * 5,
        scratch_shapes=[
            pltpu.VMEM((feat // LANES, rows, res, LANES), F32),
            pltpu.VMEM((res // pack, rows, LANES), BF),
            pltpu.VMEM((heads, trows, tcols), BF),
            pltpu.VMEM((pack, LANES, feat), BF),
            pltpu.VMEM((rows * tiles, prod * tcols), BF),
            pltpu.VMEM((cz, prod * prod), BF),
            dma((cols,)),
            dma((cols,)),
            dma((n * cols,)),
            dma((tiles,)),
            dma((tiles,)),
            dma((tiles,)),
            dma((tiles,)),
            dma((n * cols,)),
        ],
        compiler_params=pltpu.CompilerParams(
            collective_id=0, has_side_effects=True, vmem_limit_bytes=48 << 20
        ),
    )(x[0], pair[0], gm[None], gp[None], gb[None], bmap.T, wl.T, wr.T, wp, gg[None], gwiden, gshrink)

    def whole(a):
        return pl.BlockSpec(a.shape, lambda i: (0,) * a.ndim)

    gf2 = gf[None]
    srows = 2
    alignment_revised = pl.pallas_call(
        functools.partial(row_kernel, heads),
        grid=(rows // srows,),
        out_shape=sds((rows, res, feat), F32),
        in_specs=[
            pl.BlockSpec((cols, srows, res, feat), lambda i: (0, i, 0, 0)),
            whole(bias),
            pl.BlockSpec((srows, res, feat), lambda i: (i, 0, 0)),
            whole(wq),
            whole(wk),
            whole(wv),
            whole(wo),
            whole(gf2),
            whole(widen),
            whole(shrink),
        ],
        out_specs=pl.BlockSpec((srows, res, feat), lambda i: (i, 0, 0)),
        scratch_shapes=[pltpu.VMEM((heads * res, res * cols), F32)],
        compiler_params=pltpu.CompilerParams(vmem_limit_bytes=48 << 20),
    )(normed, bias, x[0], wq, wk, wv, wo, gf2, widen, shrink)
    return alignment_revised[None], grid_revised[None]


def solution(mesh):
    placed = (
        P(("groups", "branch"), "tile", "col", None),
        P(("groups", "branch"), "tile", "col", None),
        P(),
        P(),
        P(),
        P(),
        P(),
        P(),
        P(),
        P(),
        P(),
        P(),
        P(),
        P(),
        P(),
        P(),
        P(),
        P(),
        P(),
    )
    return jax.shard_map(
        functools.partial(on_device, mesh.shape["tile"], mesh.shape["col"]),
        mesh=mesh,
        in_specs=placed,
        out_specs=(
            P(("groups", "branch"), "tile", "col", None),
            P(("groups", "branch"), "tile", "col", None),
        ),
        check_vma=False,
    )
```
